256 devices in a mesh: sta: 32 (over z, y_lo, core), hr: 8 (over x, y_hi).
Axes of the slice: x: 4, y: 4 (y_hi: 2, y_lo: 2; y = y_hi * 2 + y_lo), z: 8, core: 2. Of those that a mesh axis runs over, the one named last changes fastest.
Arguments:
- spectra: bfloat16 [2048, 48, 2, 2048], P('sta', 'hr'), may hold values from -640 to 640, as said below
- pair_list: int32 [32, 2, 128], P('sta'), may hold values from 0 to 191, as said below
- pair_count: int32 [32], P('sta'), may hold values from 16 to 128, as said below
Outputs:
- correlation: float32 [4096, 2432], P(('sta', 'hr'))
The draws below stay inside these ranges and needn't reach their ends.
Inputs may be any that keep to these rules, and one draw needn't show every extreme that they name: `spectra`: raw spectral values. `pair_list`: entries of used slots: the first lies below 64, the second differs from the first; slots at or past the block's count hold 0. In a block that uses all 128 slots, the second entries name every one of 64 .. 191. `pair_count`: some block uses all 128 slots.
All inputs are finite; a program needn't handle non-finite values.
Results may differ from the reference program's by a relative error of at most 0.0041.
Values may be sent and summed in bfloat16 or wider, within the bound.
No kernel may reach another device: no remote copies, remote signals or barrier semaphores. Data moves between devices by JAX's collectives and lax.ppermute only.
A program may use at most 192 MiB of HBM per device.

```python
import math
import jax
import jax.numpy as jnp
from jax import lax

S_DEV = 64
F = 2048
BAND = 128
HALF = 1216
SAMPLES = 36000
K0 = 90
P_CAP = 128
LAGS = 2432
STATIONS = 2048
SEGMENTS = 48
PAIRS = 4096
N_STA = 32


def pair_tables(key):
    key_first = jax.random.fold_in(key, 11)
    key_step = jax.random.fold_in(key, 12)
    key_count = jax.random.fold_in(key, 13)
    key_busy = jax.random.fold_in(key, 14)
    key_cover = jax.random.fold_in(key, 15)
    first_index = jax.random.randint(key_first, (N_STA, P_CAP), 0, S_DEV)
    step_index = jax.random.randint(key_step, (N_STA, P_CAP), 1, 3 * S_DEV)
    second_index = jnp.remainder(first_index + step_index, 3 * S_DEV)
    counts = jax.random.randint(key_count, (N_STA,), P_CAP // 8, P_CAP // 2 + 1)
    busiest = jax.random.randint(key_busy, (), 0, N_STA)
    counts = jnp.where(jnp.arange(N_STA) == busiest, P_CAP, counts)
    cover_order = jax.random.permutation(key_cover, 2 * S_DEV).astype(jnp.int32)
    cover_slots = S_DEV + jnp.take(cover_order, jnp.remainder(jnp.arange(P_CAP, dtype=jnp.int32), 2 * S_DEV))
    is_busiest = (jnp.arange(N_STA) == busiest)[:, None]
    second_index = jnp.where(is_busiest, cover_slots[None, :], second_index)
    live_rows = jnp.arange(P_CAP)[None, :] < counts[:, None]
    first_index = jnp.where(live_rows, first_index, 0)
    second_index = jnp.where(live_rows, second_index, 0)
    return (jnp.stack([first_index, second_index], axis=1).astype(jnp.int32), counts.astype(jnp.int32))


def draw_pair_list(key, part):
    return pair_tables(key)[0]


def draw_pair_count(key, part):
    return pair_tables(key)[1]


def draw_spectra(key, part):
    key_value = jax.random.fold_in(key, 21)
    key_bin = jax.random.fold_in(key, 22)
    full_shape = (STATIONS, SEGMENTS, 2, F)
    bin_scale = jnp.exp(jax.random.uniform(key_bin, (STATIONS, SEGMENTS, 1, F)) * math.log(10.0))
    values = jnp.clip(jax.random.normal(key_value, full_shape), -4.0, 4.0) * bin_scale
    return values.astype(jnp.float32).astype(jnp.bfloat16)


def setup_inputs(seed: int = 0) -> dict:
    key_list = jax.random.split(jax.random.key(seed), 4)
    spectra = draw_spectra(jax.random.fold_in(key_list[3], 71), 0)
    pair_list = draw_pair_list(jax.random.fold_in(key_list[3], 71), 0)
    pair_count = draw_pair_count(jax.random.fold_in(key_list[3], 71), 0)
    return dict(spectra=spectra, pair_list=pair_list, pair_count=pair_count)


def whiten(spectra):
    stations, segments, halves, freq_bins = spectra.shape
    grouped = spectra.astype(jnp.float32).reshape(stations, segments, halves, freq_bins // BAND, BAND)
    band_power = lax.optimization_barrier(jnp.sum(grouped * grouped, axis=(2, 4), keepdims=True)) / BAND
    return (grouped * lax.rsqrt(band_power + 1e-06)).reshape(spectra.shape).astype(jnp.bfloat16)

def lag_table():
    freq_index = K0 + jnp.arange(F, dtype=jnp.int32)
    lag_index = jnp.arange(LAGS, dtype=jnp.int32) - HALF
    phase_turns = jnp.remainder(freq_index[:, None] * lag_index[None, :], SAMPLES)
    angles = phase_turns.astype(jnp.float32) * (2.0 * math.pi / SAMPLES)
    return jnp.concatenate([jnp.cos(angles), -jnp.sin(angles)], axis=0)

def cross_tile(buffer, first_index, second_index, live_rows):
    left_spec = jnp.take(buffer, first_index, axis=0)
    right_spec = jnp.take(buffer, second_index, axis=0)
    left_re = left_spec[:, :, 0].astype(jnp.float32)
    left_im = left_spec[:, :, 1].astype(jnp.float32)
    right_re = right_spec[:, :, 0].astype(jnp.float32)
    right_im = right_spec[:, :, 1].astype(jnp.float32)
    cross_re = lax.optimization_barrier(jnp.sum(left_re * right_re + left_im * right_im, axis=1))
    cross_im = lax.optimization_barrier(jnp.sum(left_im * right_re - left_re * right_im, axis=1))
    return jnp.concatenate([cross_re, cross_im], axis=-1) * live_rows[:, None]

def reference(spectra, pair_list, pair_count):
    blocks = spectra.reshape(N_STA, S_DEV, SEGMENTS, 2, F)
    phase_table = lag_table()
    norm_scale = 1.0 / math.sqrt(SEGMENTS * F)

    def one_block(block_args):
        block_id, pairs, live_count = block_args
        own_block = whiten(blocks[block_id])
        prev_one = whiten(blocks[jnp.remainder(block_id - 1, N_STA)])
        prev_two = whiten(blocks[jnp.remainder(block_id - 2, N_STA)])
        buffer = jnp.concatenate([own_block, prev_one, prev_two], axis=0)
        live_rows = (jnp.arange(P_CAP, dtype=jnp.int32) < live_count).astype(jnp.float32)
        cross = cross_tile(buffer, pairs[0], pairs[1], live_rows)
        return jnp.dot(cross, phase_table, precision=lax.Precision.HIGHEST, preferred_element_type=jnp.float32) * norm_scale
    stacked = lax.map(one_block, (jnp.arange(N_STA, dtype=jnp.int32), pair_list, pair_count))
    return stacked.reshape(PAIRS, LAGS)
```

```python
import functools
import math

import jax
import jax.numpy as jnp
import numpy as np
from jax import lax
from jax.experimental import pallas as pl
from jax.experimental.pallas import tpu as pltpu
from jax.sharding import Mesh
from jax.sharding import PartitionSpec as P
import ml_dtypes

F = 2048
BAND = 128
HALF = 1216
SAMPLES = 36000
K0 = 90
LAGS = 2432
SEGS = 6
CHUNKS = 2
PARTS = 4
WIDE = F // CHUNKS
PIECE = WIDE // PARTS
BANDS = PIECE // BAND
ROWS = 16


def whiten_kernel(me_ref, x_ref, *out_refs):
    for m in range(PARTS):
        start = pl.multiple_of((me_ref[0] ^ m) * PIECE, PIECE)
        for s in range(SEGS):
            x = x_ref[:, s, :, pl.ds(start, PIECE)].astype(jnp.float32)
            re = x[:, 0, :]
            im = x[:, 1, :]
            for b in range(BANDS):
                a = re[:, b * BAND : (b + 1) * BAND]
                c = im[:, b * BAND : (b + 1) * BAND]
                power = jnp.sum(a * a + c * c, axis=-1, keepdims=True) / BAND
                gain = lax.rsqrt(power + 1e-06)
                lane = 2 * s * PIECE + b * BAND
                out_refs[m][:, lane : lane + BAND] = (a * gain).astype(jnp.bfloat16)
                lane += PIECE
                out_refs[m][:, lane : lane + BAND] = (c * gain).astype(jnp.bfloat16)


def whiten(me, spectra, chunk):
    stations = spectra.shape[0]
    width = 2 * SEGS * PIECE
    return pl.pallas_call(
        whiten_kernel,
        grid_spec=pltpu.PrefetchScalarGridSpec(
            num_scalar_prefetch=1,
            grid=(stations // ROWS,),
            in_specs=[pl.BlockSpec((ROWS, SEGS, 2, WIDE), lambda i, me: (i, 0, 0, chunk))],
            out_specs=[pl.BlockSpec((ROWS, width), lambda i, me: (i, 0))] * PARTS,
        ),
        out_shape=[jax.ShapeDtypeStruct((stations, width), jnp.bfloat16)] * PARTS,
        name="whiten",
    )(me, spectra)


def pair_kernel(me_ref, rows_ref, *refs):
    sources, out_ref, held, sems = refs[:6], refs[6], refs[7], refs[8]
    me = me_ref[0]
    core = me & 1
    places = [2 + (me ^ m) for m in range(PARTS)] + [core, 1 - core]
    copies = []
    for n, (source, place) in enumerate(zip(sources, places)):
        start = pl.multiple_of(place * 64, 64)
        copies.append(pltpu.make_async_copy(source, held.at[pl.ds(start, 64)], sems.at[n]))
        copies[-1].start()
    for copy in copies:
        copy.wait()
    for j in range(PARTS):
        column = lax.broadcasted_iota(jnp.int32, (256, 192), 1)
        pick = jnp.where(rows_ref[j] == column, 1.0, 0.0).astype(jnp.bfloat16)
        cross_re = jnp.zeros((128, PIECE), jnp.float32)
        cross_im = jnp.zeros((128, PIECE), jnp.float32)
        for s in range(SEGS):
            taken = jnp.dot(
                pick,
                held[j * 64 : j * 64 + 192, 2 * s * PIECE : 2 * (s + 1) * PIECE],
                preferred_element_type=jnp.float32,
            )
            a_re, a_im = taken[:128, :PIECE], taken[:128, PIECE:]
            b_re, b_im = taken[128:, :PIECE], taken[128:, PIECE:]
            cross_re += a_re * b_re + a_im * b_im
            cross_im += a_im * b_re - a_re * b_im
        out_ref[j, :, :PIECE] = cross_re.astype(out_ref.dtype)
        out_ref[j, :, PIECE:] = cross_im.astype(out_ref.dtype)


def pair_products(me, rows, sources):
    width = 2 * SEGS * PIECE
    return pl.pallas_call(
        pair_kernel,
        in_specs=[
            pl.BlockSpec(memory_space=pltpu.SMEM),
            pl.BlockSpec(memory_space=pltpu.VMEM),
        ]
        + [pl.BlockSpec(memory_space=pl.ANY)] * 6,
        out_specs=pl.BlockSpec(memory_space=pltpu.VMEM),
        out_shape=jax.ShapeDtypeStruct((PARTS, 128, 2 * PIECE), jnp.bfloat16),
        scratch_shapes=[
            pltpu.VMEM((6 * 64, width), jnp.bfloat16),
            pltpu.SemaphoreType.DMA((6,)),
        ],
        compiler_params=pltpu.CompilerParams(vmem_limit_bytes=32 * 1024 * 1024),
        name="pair_products",
    )(me, rows, *sources)


def lag_table():
    freq = np.arange(F, dtype=np.int64).reshape(CHUNKS, PARTS, PIECE)
    lag = np.arange(LAGS, dtype=np.int64) - HALF
    turns = np.remainder((K0 + freq)[..., None] * lag, SAMPLES)
    angles = turns * (2.0 * math.pi / SAMPLES)
    table = np.stack([np.cos(angles), -np.sin(angles)], axis=2)
    return table.reshape(2 * F, LAGS).astype(ml_dtypes.bfloat16)


def on_device(table, spectra, pair_list, pair_count):
    y, c = lax.axis_index("y"), lax.axis_index("c")
    me = (2 * y + c).reshape(1).astype(jnp.int32)
    z_count = lax.axis_size("z")
    z_pairs = [(n, (n + 1) % z_count) for n in range(z_count)]
    live = jnp.arange(128, dtype=jnp.int32)[None, None] < pair_count[:, None, None]
    first = 128 + pair_list[:, 0:1]
    second = pair_list[:, 1:2]
    second = jnp.where(second < 64, second + 128, jnp.where(second < 128, second, second - 128))
    rows = jnp.where(live, jnp.concatenate([first, second], axis=1), -1)
    rows = lax.all_gather(rows, ("y", "c"), axis=0, tiled=True).reshape(PARTS, 256, 1)

    received = []
    for chunk in range(CHUNKS):
        pieces = whiten(me, spectra, chunk)
        blocks = [pieces[0]] + [
            lax.ppermute(pieces[m], ("y", "c"), [(n, n ^ m) for n in range(PARTS)]) for m in (1, 2, 3)
        ]
        behind = [jnp.where(y == 1, blocks[m], blocks[m + 2]) for m in (0, 1)]
        blocks += [lax.ppermute(block, "z", z_pairs) for block in behind]
        cross = pair_products(me, rows, blocks)
        cross = cross.reshape(PARTS * 128, 2 * PIECE)
        got = lax.all_to_all(cross, ("y", "c", "h"), 0, 0, tiled=True)
        got = got.reshape(PARTS, 8, 16, 2 * PIECE).astype(jnp.float32)
        received.append(jnp.sum(got, axis=1))
    total = jnp.stack(received).reshape(2 * F // (2 * PIECE), 16, 2 * PIECE)
    total = jnp.transpose(total, (1, 0, 2)).reshape(16, 2 * F).astype(jnp.bfloat16)
    scale = 1.0 / math.sqrt(48 * F)
    return jnp.dot(total, table, preferred_element_type=jnp.float32) * scale


def solution(mesh):
    inner = Mesh(mesh.devices.reshape(-1, 2, 2, 8), ("z", "y", "c", "h"))
    sta = ("z", "y", "c")
    table = lag_table()

    def run(spectra, pair_list, pair_count):
        return jax.shard_map(
            on_device,
            mesh=inner,
            in_specs=(P(), P(sta, "h", None, None), P(sta, None, None), P(sta)),
            out_specs=P(sta + ("h",), None),
            check_vma=False,
        )(jnp.asarray(table), spectra, pair_list, pair_count)

    return run
```

```python
import functools
import math

import jax
import jax.numpy as jnp
import numpy as np
from jax import lax
from jax.experimental import pallas as pl
from jax.experimental.pallas import tpu as pltpu
from jax.sharding import Mesh
from jax.sharding import PartitionSpec as P
import ml_dtypes

F = 2048
BAND = 128
HALF = 1216
SAMPLES = 36000
K0 = 90
LAGS = 2432
SEGS = 6
CHUNKS = 2
PARTS = 4
WIDE = F // CHUNKS
PIECE = WIDE // PARTS
BANDS = PIECE // BAND
ROWS = 16
SPAN = 256
TURNS = -(-LAGS // SPAN)


def whiten_kernel(me_ref, x_ref, *out_refs):
    for m in range(PARTS):
        start = pl.multiple_of((me_ref[0] ^ m) * PIECE, PIECE)
        for s in range(SEGS):
            x = x_ref[:, s, :, pl.ds(start, PIECE)].astype(jnp.float32)
            re = x[:, 0, :]
            im = x[:, 1, :]
            for b in range(BANDS):
                a = re[:, b * BAND : (b + 1) * BAND]
                c = im[:, b * BAND : (b + 1) * BAND]
                power = jnp.sum(a * a + c * c, axis=-1, keepdims=True) / BAND
                gain = lax.rsqrt(power + 1e-06)
                lane = 2 * s * PIECE + b * BAND
                out_refs[m][:, lane : lane + BAND] = (a * gain).astype(jnp.bfloat16)
                lane += PIECE
                out_refs[m][:, lane : lane + BAND] = (c * gain).astype(jnp.bfloat16)


def whiten(me, spectra, chunk):
    stations = spectra.shape[0]
    width = 2 * SEGS * PIECE
    return pl.pallas_call(
        whiten_kernel,
        grid_spec=pltpu.PrefetchScalarGridSpec(
            num_scalar_prefetch=1,
            grid=(stations // ROWS,),
            in_specs=[pl.BlockSpec((ROWS, SEGS, 2, WIDE), lambda i, me: (i, 0, 0, chunk))],
            out_specs=[pl.BlockSpec((ROWS, width), lambda i, me: (i, 0))] * PARTS,
        ),
        out_shape=[jax.ShapeDtypeStruct((stations, width), jnp.bfloat16)] * PARTS,
        name="whiten",
    )(me, spectra)


def pair_kernel(me_ref, pick_ref, *refs):
    *near_refs, behind_ref, out_ref, held, sems = refs
    sources = list(near_refs) + [behind_ref.at[0], behind_ref.at[1]]
    me = me_ref[0]
    core = me & 1
    places = [2 + (me ^ m) for m in range(PARTS)] + [core, 1 - core]
    copies = []
    for n, (source, place) in enumerate(zip(sources, places)):
        start = pl.multiple_of(place * 64, 64)
        copies.append(pltpu.make_async_copy(source, held.at[pl.ds(start, 64)], sems.at[n]))
        copies[-1].start()
    for copy in copies:
        copy.wait()
    for j in range(PARTS):
        pick = pick_ref[j ^ me]
        cross_re = jnp.zeros((128, PIECE), jnp.float32)
        cross_im = jnp.zeros((128, PIECE), jnp.float32)
        for s in range(SEGS):
            taken = jnp.dot(
                pick,
                held[j * 64 : j * 64 + 192, 2 * s * PIECE : 2 * (s + 1) * PIECE],
                preferred_element_type=jnp.float32,
            )
            a_re, a_im = taken[:128, :PIECE], taken[:128, PIECE:]
            b_re, b_im = taken[128:, :PIECE], taken[128:, PIECE:]
            cross_re += a_re * b_re + a_im * b_im
            cross_im += a_im * b_re - a_re * b_im
        out_ref[j, :, :PIECE] = cross_re.astype(out_ref.dtype)
        out_ref[j, :, PIECE:] = cross_im.astype(out_ref.dtype)


def pair_products(me, picks, sources):
    width = 2 * SEGS * PIECE
    return pl.pallas_call(
        pair_kernel,
        in_specs=[
            pl.BlockSpec(memory_space=pltpu.SMEM),
            pl.BlockSpec(memory_space=pltpu.VMEM),
        ]
        + [pl.BlockSpec(memory_space=pltpu.HBM)] * 5,
        out_specs=pl.BlockSpec(memory_space=pltpu.VMEM),
        out_shape=jax.ShapeDtypeStruct((PARTS, 128, 2 * PIECE), jnp.bfloat16),
        scratch_shapes=[
            pltpu.VMEM((6 * 64, width), jnp.bfloat16),
            pltpu.SemaphoreType.DMA((6,)),
        ],
        compiler_params=pltpu.CompilerParams(vmem_limit_bytes=32 * 1024 * 1024),
        name="pair_products",
    )(me, picks, *sources)


def lag_kernel(cos_ref, sin_ref, table_ref, *refs):
    got_refs, out_ref = refs[:-1], refs[-1]
    total = jnp.zeros((16 * TURNS, SPAN), jnp.float32)
    for g, got_ref in enumerate(got_refs):
        for j in range(PARTS):
            cross = got_ref[8 * j].astype(jnp.float32)
            for h in range(1, 8):
                cross += got_ref[8 * j + h].astype(jnp.float32)
            re, im = cross[:, :PIECE], cross[:, PIECE:]
            bins = slice((g * PARTS + j) * PIECE, (g * PARTS + j + 1) * PIECE)
            turned_re, turned_im = [], []
            for r in range(TURNS):
                cos, sin = cos_ref[r : r + 1, bins], sin_ref[r : r + 1, bins]
                turned_re.append(re * cos - im * sin)
                turned_im.append(re * sin + im * cos)
            for k, turned in enumerate((turned_re, turned_im)):
                start = (2 * (g * PARTS + j) + k) * PIECE
                total += jnp.dot(
                    jnp.concatenate(turned).astype(jnp.bfloat16),
                    table_ref[start : start + PIECE],
                    preferred_element_type=jnp.float32,
                )
    total = total * (1.0 / math.sqrt(48 * F))
    for r in range(TURNS):
        width = min(SPAN, LAGS - r * SPAN)
        out_ref[:, r * SPAN : r * SPAN + width] = total[16 * r : 16 * (r + 1), :width]


def lag_sums(tables, got):
    return pl.pallas_call(
        lag_kernel,
        out_shape=jax.ShapeDtypeStruct((16, LAGS), jnp.float32),
        compiler_params=pltpu.CompilerParams(vmem_limit_bytes=32 * 1024 * 1024),
        name="lag_sums",
    )(*tables, *got)


def angles(freq, lag):
    turns = np.remainder((K0 + freq) * lag, SAMPLES)
    return turns * (2.0 * math.pi / SAMPLES)


def lag_tables():
    freq = np.arange(F, dtype=np.int64)
    turn = angles(freq, SPAN * np.arange(TURNS, dtype=np.int64)[:, None])
    near = angles(freq[:, None], np.arange(SPAN, dtype=np.int64) - HALF)
    near = near.reshape(CHUNKS * PARTS, PIECE, SPAN)
    table = np.stack([np.cos(near), -np.sin(near)], axis=1).reshape(2 * F, SPAN)
    return (
        np.cos(turn).astype(np.float32),
        np.sin(turn).astype(np.float32),
        table.astype(ml_dtypes.bfloat16),
    )


def on_device(tables, spectra, pair_list, pair_count):
    y, c = lax.axis_index("y"), lax.axis_index("c")
    me = (2 * y + c).reshape(1).astype(jnp.int32)
    z_count = lax.axis_size("z")
    z_pairs = [(n, (n + 1) % z_count) for n in range(z_count)]
    live = jnp.arange(128, dtype=jnp.int32)[None, None] < pair_count[:, None, None]
    first = 128 + pair_list[:, 0:1]
    second = pair_list[:, 1:2]
    second = jnp.where(second < 64, second + 128, jnp.where(second < 128, second, second - 128))
    rows = jnp.where(live, jnp.concatenate([first, second], axis=1), -1)
    yc_pairs = [[(n, n ^ m) for n in range(PARTS)] for m in range(PARTS)]
    rows = rows.reshape(1, 256)
    spectra, rows = lax.optimization_barrier((spectra, rows))
    near = [rows] + [lax.ppermute(rows, ("y", "c"), yc_pairs[m]) for m in (1, 2, 3)]
    column = jnp.arange(192, dtype=jnp.int32)
    picks = (jnp.concatenate(near)[:, :, None] == column).astype(jnp.bfloat16)

    arrived = []
    for chunk in range(CHUNKS):
        pieces = whiten(me, spectra, chunk)
        if chunk == 0:
            pieces, picks = lax.optimization_barrier((pieces, picks))
        arrived.append(
            [pieces[0]] + [lax.ppermute(pieces[m], ("y", "c"), yc_pairs[m]) for m in (2, 3, 1)]
        )
    moved, behind = [], []
    for own, far, cross, side in arrived:
        ahead = [jnp.where(y == 1, own, far), jnp.where(y == 1, side, cross)]
        moved.append(jnp.stack(ahead))
        behind.append(lax.ppermute(moved[-1], "z", z_pairs))
    got = []
    for chunk in range(CHUNKS):
        own, far, cross, side = arrived[chunk]
        product = pair_products(me, picks, [own, side, far, cross, behind[chunk]])
        product = product.reshape(PARTS * 128, 2 * PIECE)
        if chunk == 0:
            product, _ = lax.optimization_barrier((product, moved[1]))
        got.append(lax.all_to_all(product, ("y", "c", "h"), 0, 0, tiled=True).reshape(32, 16, 2 * PIECE))
    return lag_sums(tables, got)


def solution(mesh):
    inner = Mesh(mesh.devices.reshape(-1, 2, 2, 8), ("z", "y", "c", "h"))
    sta = ("z", "y", "c")
    tables = lag_tables()

    def run(spectra, pair_list, pair_count):
        return jax.shard_map(
            on_device,
            mesh=inner,
            in_specs=((P(),) * 3, P(sta, "h", None, None), P(sta, None, None), P(sta)),
            out_specs=P(sta + ("h",), None),
            check_vma=False,
        )(tuple(jnp.asarray(table) for table in tables), spectra, pair_list, pair_count)

    return run
```

```python
import functools
import math

import jax
import jax.numpy as jnp
import numpy as np
from jax import lax
from jax.experimental import pallas as pl
from jax.experimental.pallas import tpu as pltpu
from jax.sharding import Mesh
from jax.sharding import PartitionSpec as P
import ml_dtypes

F = 2048
BAND = 128
HALF = 1216
SAMPLES = 36000
K0 = 90
LAGS = 2432
SEGS = 6
CHUNKS = 2
PARTS = 4
WIDE = F // CHUNKS
PIECE = WIDE // PARTS
BANDS = PIECE // BAND
ROWS = 16
SPAN = 256
TURNS = -(-LAGS // SPAN)


def whiten_kernel(me_ref, x_ref, *out_refs):
    for m in range(PARTS):
        start = pl.multiple_of((me_ref[0] ^ m) * PIECE, PIECE)
        for s in range(SEGS):
            x = x_ref[:, s, :, pl.ds(start, PIECE)].astype(jnp.float32)
            re = x[:, 0, :]
            im = x[:, 1, :]
            for b in range(BANDS):
                a = re[:, b * BAND : (b + 1) * BAND]
                c = im[:, b * BAND : (b + 1) * BAND]
                power = jnp.sum(a * a + c * c, axis=-1, keepdims=True) / BAND
                gain = lax.rsqrt(power + 1e-06)
                lane = 2 * s * PIECE + b * BAND
                out_refs[m][:, lane : lane + BAND] = (a * gain).astype(jnp.bfloat16)
                lane += PIECE
                out_refs[m][:, lane : lane + BAND] = (c * gain).astype(jnp.bfloat16)


def whiten(me, spectra, chunk):
    stations = spectra.shape[0]
    width = 2 * SEGS * PIECE
    return pl.pallas_call(
        whiten_kernel,
        grid_spec=pltpu.PrefetchScalarGridSpec(
            num_scalar_prefetch=1,
            grid=(stations // ROWS,),
            in_specs=[pl.BlockSpec((ROWS, SEGS, 2, WIDE), lambda i, me: (i, 0, 0, chunk))],
            out_specs=[pl.BlockSpec((ROWS, width), lambda i, me: (i, 0))] * PARTS,
        ),
        out_shape=[jax.ShapeDtypeStruct((stations, width), jnp.bfloat16)] * PARTS,
        name="whiten",
    )(me, spectra)


def pair_kernel(numbers, me_ref, pick_ref, *refs):
    *sources, out_ref, held, sems = refs
    me = me_ref[0]
    places = [1 + (me ^ m) for m in range(PARTS)] + [0, 5]
    copies = []
    for n, (source, place) in enumerate(zip(sources, places)):
        start = pl.multiple_of(place * 64, 64)
        copies.append(pltpu.make_async_copy(source, held.at[pl.ds(start, 64)], sems.at[n]))
        copies[-1].start()
    for copy in copies:
        copy.wait()
    for n, j in enumerate(numbers):
        if j == 0:
            pick, rows = pick_ref[me, :, 64:], slice(0, 128)
        else:
            pick = pick_ref[j ^ me if j < PARTS else PARTS]
            rows = slice((j - 1) * 64, (j + 2) * 64)
        cross_re = jnp.zeros((128, PIECE), jnp.float32)
        cross_im = jnp.zeros((128, PIECE), jnp.float32)
        for s in range(SEGS):
            taken = jnp.dot(
                pick,
                held[rows, 2 * s * PIECE : 2 * (s + 1) * PIECE],
                preferred_element_type=jnp.float32,
            )
            a_re, a_im = taken[:128, :PIECE], taken[:128, PIECE:]
            b_re, b_im = taken[128:, :PIECE], taken[128:, PIECE:]
            cross_re += a_re * b_re + a_im * b_im
            cross_im += a_im * b_re - a_re * b_im
        out_ref[n, :, :PIECE] = cross_re.astype(out_ref.dtype)
        out_ref[n, :, PIECE:] = cross_im.astype(out_ref.dtype)


def pair_products(numbers, me, picks, sources):
    width = 2 * SEGS * PIECE
    return pl.pallas_call(
        functools.partial(pair_kernel, numbers),
        in_specs=[
            pl.BlockSpec(memory_space=pltpu.SMEM),
            pl.BlockSpec(memory_space=pltpu.VMEM),
        ]
        + [pl.BlockSpec(memory_space=pltpu.HBM)] * 6,
        out_specs=pl.BlockSpec(memory_space=pltpu.VMEM),
        out_shape=jax.ShapeDtypeStruct((len(numbers), 128, 2 * PIECE), jnp.bfloat16),
        scratch_shapes=[
            pltpu.VMEM((6 * 64, width), jnp.bfloat16),
            pltpu.SemaphoreType.DMA((6,)),
        ],
        compiler_params=pltpu.CompilerParams(vmem_limit_bytes=32 * 1024 * 1024),
        name="pair_products",
    )(me, picks, *sources)


def lag_kernel(cos_ref, sin_ref, table_ref, *refs):
    got_refs, out_ref = refs[:-1], refs[-1]
    total = jnp.zeros((16 * TURNS, SPAN), jnp.float32)
    for g, got_ref in enumerate(got_refs):
        for j in range(PARTS):
            cross = got_ref[8 * j].astype(jnp.float32)
            for h in range(1, 8):
                cross += got_ref[8 * j + h].astype(jnp.float32)
            re, im = cross[:, :PIECE], cross[:, PIECE:]
            bins = slice((g * PARTS + j) * PIECE, (g * PARTS + j + 1) * PIECE)
            turned_re, turned_im = [], []
            for r in range(TURNS):
                cos, sin = cos_ref[r : r + 1, bins], sin_ref[r : r + 1, bins]
                turned_re.append(re * cos - im * sin)
                turned_im.append(re * sin + im * cos)
            for k, turned in enumerate((turned_re, turned_im)):
                start = (2 * (g * PARTS + j) + k) * PIECE
                total += jnp.dot(
                    jnp.concatenate(turned).astype(jnp.bfloat16),
                    table_ref[start : start + PIECE],
                    preferred_element_type=jnp.float32,
                )
    total = total * (1.0 / math.sqrt(48 * F))
    for r in range(TURNS):
        width = min(SPAN, LAGS - r * SPAN)
        out_ref[:, r * SPAN : r * SPAN + width] = total[16 * r : 16 * (r + 1), :width]


def lag_sums(tables, got):
    return pl.pallas_call(
        lag_kernel,
        out_shape=jax.ShapeDtypeStruct((16, LAGS), jnp.float32),
        compiler_params=pltpu.CompilerParams(vmem_limit_bytes=32 * 1024 * 1024),
        name="lag_sums",
    )(*tables, *got)


def angles(freq, lag):
    turns = np.remainder((K0 + freq) * lag, SAMPLES)
    return turns * (2.0 * math.pi / SAMPLES)


def lag_tables():
    freq = np.arange(F, dtype=np.int64)
    turn = angles(freq, SPAN * np.arange(TURNS, dtype=np.int64)[:, None])
    near = angles(freq[:, None], np.arange(SPAN, dtype=np.int64) - HALF)
    near = near.reshape(CHUNKS * PARTS, PIECE, SPAN)
    table = np.stack([np.cos(near), -np.sin(near)], axis=1).reshape(2 * F, SPAN)
    return (
        np.cos(turn).astype(np.float32),
        np.sin(turn).astype(np.float32),
        table.astype(ml_dtypes.bfloat16),
    )


def on_device(tables, spectra, pair_list, pair_count):
    y, c = lax.axis_index("y"), lax.axis_index("c")
    me = (2 * y + c).reshape(1).astype(jnp.int32)
    z_count = lax.axis_size("z")
    z_up = [(n, (n + 1) % z_count) for n in range(z_count)]
    z_down = [((n + 1) % z_count, n) for n in range(z_count)]
    live = jnp.arange(128, dtype=jnp.int32)[None, None] < pair_count[:, None, None]
    first = 128 + pair_list[:, 0:1]
    second = pair_list[:, 1:2]
    second = jnp.where(second < 64, second + 128, jnp.where(second < 128, second, second - 128))
    rows = jnp.where(live, jnp.concatenate([first, second], axis=1), -1)
    yc_pairs = [[(n, n ^ m) for n in range(PARTS)] for m in range(PARTS)]
    rows = rows.reshape(1, 256)
    spectra, rows = lax.optimization_barrier((spectra, rows))
    near = [rows] + [lax.ppermute(rows, ("y", "c"), yc_pairs[m]) for m in (1, 2, 3)]
    near = jnp.concatenate(near)
    above = lax.ppermute(lax.dynamic_slice_in_dim(near, me[0], 1, 0), "z", z_down)
    is_first = (jnp.arange(256) < 128)[None]
    above = jnp.where(is_first | (above < 64), above, -1)
    column = jnp.arange(192, dtype=jnp.int32)
    picks = (jnp.concatenate([near, above])[:, :, None] == column).astype(jnp.bfloat16)

    arrived = []
    for chunk in range(CHUNKS):
        pieces = whiten(me, spectra, chunk)
        if chunk == 0:
            pieces, near = lax.optimization_barrier((pieces, near))
        arrived.append(
            [pieces[0]] + [lax.ppermute(pieces[m], ("y", "c"), yc_pairs[m]) for m in (2, 3, 1)]
        )
    crossed, moved = [], []
    for own, far, cross, side in arrived:
        blocks = [own, side, far, cross]
        top = jnp.where(y == 1, jnp.where(c == 1, own, side), jnp.where(c == 1, far, cross))
        low = jnp.where(y == 0, jnp.where(c == 0, own, side), jnp.where(c == 0, far, cross))
        moved.append(top)
        crossed.append(blocks + [lax.ppermute(top, "z", z_up), lax.ppermute(low, "z", z_down)])
    got = []
    for chunk in range(CHUNKS):
        other = pair_products((PARTS,), me, picks, crossed[chunk])
        below = lax.ppermute(other, "z", z_up)
        picks, other = lax.optimization_barrier((picks, other))
        product = pair_products(tuple(range(PARTS)), me, picks, crossed[chunk])
        product = product + jnp.pad(below, ((0, PARTS - 1), (0, 0), (0, 0)))
        product = product.reshape(PARTS * 128, 2 * PIECE)
        if chunk == 0:
            product, _ = lax.optimization_barrier((product, moved[1]))
        got.append(lax.all_to_all(product, ("y", "c", "h"), 0, 0, tiled=True).reshape(32, 16, 2 * PIECE))
    return lag_sums(tables, got)


def solution(mesh):
    inner = Mesh(mesh.devices.reshape(-1, 2, 2, 8), ("z", "y", "c", "h"))
    sta = ("z", "y", "c")
    tables = lag_tables()

    def run(spectra, pair_list, pair_count):
        return jax.shard_map(
            on_device,
            mesh=inner,
            in_specs=((P(),) * 3, P(sta, "h", None, None), P(sta, None, None), P(sta)),
            out_specs=P(sta + ("h",), None),
            check_vma=False,
        )(tuple(jnp.asarray(table) for table in tables), spectra, pair_list, pair_count)

    return run
```

```python
import functools
import math

import jax
import jax.numpy as jnp
import numpy as np
from jax import lax
from jax.experimental import pallas as pl
from jax.experimental.pallas import tpu as pltpu
from jax.sharding import Mesh
from jax.sharding import PartitionSpec as P
import ml_dtypes

F = 2048
BAND = 128
HALF = 1216
SAMPLES = 36000
K0 = 90
LAGS = 2432
SEGS = 6
CHUNKS = 2
PARTS = 4
WIDE = F // CHUNKS
PIECE = WIDE // PARTS
BANDS = PIECE // BAND
ROWS = 16
SPAN = 128
TURNS = -(-LAGS // SPAN)


def whiten_kernel(me_ref, x_ref, *out_refs):
    for m in range(PARTS):
        start = pl.multiple_of((me_ref[0] ^ m) * PIECE, PIECE)
        for s in range(SEGS):
            x = x_ref[:, s, :, pl.ds(start, PIECE)].astype(jnp.float32)
            re = x[:, 0, :]
            im = x[:, 1, :]
            for b in range(BANDS):
                a = re[:, b * BAND : (b + 1) * BAND]
                c = im[:, b * BAND : (b + 1) * BAND]
                power = jnp.sum(a * a + c * c, axis=-1, keepdims=True) / BAND
                gain = lax.rsqrt(power + 1e-06)
                lane = 2 * s * PIECE + b * BAND
                out_refs[m][:, lane : lane + BAND] = (a * gain).astype(jnp.bfloat16)
                lane += PIECE
                out_refs[m][:, lane : lane + BAND] = (c * gain).astype(jnp.bfloat16)


def whiten(me, spectra, chunk):
    stations = spectra.shape[0]
    width = 2 * SEGS * PIECE
    return pl.pallas_call(
        whiten_kernel,
        grid_spec=pltpu.PrefetchScalarGridSpec(
            num_scalar_prefetch=1,
            grid=(stations // ROWS,),
            in_specs=[pl.BlockSpec((ROWS, SEGS, 2, WIDE), lambda i, me: (i, 0, 0, chunk))],
            out_specs=[pl.BlockSpec((ROWS, width), lambda i, me: (i, 0))] * PARTS,
        ),
        out_shape=[jax.ShapeDtypeStruct((stations, width), jnp.bfloat16)] * PARTS,
        name="whiten",
    )(me, spectra)


def pair_kernel(numbers, me_ref, pick_ref, *refs):
    *sources, out_ref, held, sems = refs
    me = me_ref[0]
    places = [1 + (me ^ m) for m in range(PARTS)] + [0, 5]
    needed = {place for j in numbers for place in range(max(j - 1, 0), j + 2)}
    if numbers == (PARTS,):
        needed.remove(PARTS)
    copies = []
    for n, (source, place) in enumerate(zip(sources, places)):
        wanted = functools.reduce(lambda a, b: a | b, [jnp.equal(place, p) for p in sorted(needed)])
        start = pl.multiple_of(place * 64, 64)
        copies.append((wanted, pltpu.make_async_copy(source, held.at[pl.ds(start, 64)], sems.at[n])))
    for wanted, copy in copies:
        pl.when(wanted)(copy.start)
    for wanted, copy in copies:
        pl.when(wanted)(copy.wait)
    for n, j in enumerate(numbers):
        if j == 0:
            pick, rows = pick_ref[me, :, 64:], slice(0, 128)
        else:
            pick = pick_ref[j ^ me if j < PARTS else PARTS]
            rows = slice((j - 1) * 64, (j + 2) * 64)
        cross_re = jnp.zeros((128, PIECE), jnp.float32)
        cross_im = jnp.zeros((128, PIECE), jnp.float32)
        for s in range(SEGS):
            lanes = slice(2 * s * PIECE, 2 * (s + 1) * PIECE)
            if j < PARTS:
                taken = jnp.dot(pick, held[rows, lanes], preferred_element_type=jnp.float32)
            else:
                taken = jnp.concatenate(
                    [
                        jnp.dot(pick[:128, 128:], held[320:384, lanes], preferred_element_type=jnp.float32),
                        jnp.dot(pick[128:, :64], held[192:256, lanes], preferred_element_type=jnp.float32),
                    ]
                )
            a_re, a_im = taken[:128, :PIECE], taken[:128, PIECE:]
            b_re, b_im = taken[128:, :PIECE], taken[128:, PIECE:]
            cross_re += a_re * b_re + a_im * b_im
            cross_im += a_im * b_re - a_re * b_im
        out_ref[n, :, :PIECE] = cross_re.astype(out_ref.dtype)
        out_ref[n, :, PIECE:] = cross_im.astype(out_ref.dtype)


def pair_products(numbers, me, picks, sources):
    width = 2 * SEGS * PIECE
    return pl.pallas_call(
        functools.partial(pair_kernel, numbers),
        in_specs=[
            pl.BlockSpec(memory_space=pltpu.SMEM),
            pl.BlockSpec(memory_space=pltpu.VMEM),
        ]
        + [pl.BlockSpec(memory_space=pltpu.HBM)] * 6,
        out_specs=pl.BlockSpec(memory_space=pltpu.VMEM),
        out_shape=jax.ShapeDtypeStruct((len(numbers), 128, 2 * PIECE), jnp.bfloat16),
        scratch_shapes=[
            pltpu.VMEM((6 * 64, width), jnp.bfloat16),
            pltpu.SemaphoreType.DMA((6,)),
        ],
        compiler_params=pltpu.CompilerParams(vmem_limit_bytes=32 * 1024 * 1024),
        name="pair_products",
    )(me, picks, *sources)


def lag_kernel(cos_ref, sin_ref, table_ref, *refs):
    got_refs, out_ref = refs[:-1], refs[-1]
    total = jnp.zeros((16 * TURNS, SPAN), jnp.float32)
    for g, got_ref in enumerate(got_refs):
        for j in range(PARTS):
            cross = got_ref[8 * j].astype(jnp.float32)
            for h in range(1, 8):
                cross += got_ref[8 * j + h].astype(jnp.float32)
            re, im = cross[:, :PIECE], cross[:, PIECE:]
            bins = slice((g * PARTS + j) * PIECE, (g * PARTS + j + 1) * PIECE)
            turned_re, turned_im = [], []
            for r in range(TURNS):
                cos, sin = cos_ref[r : r + 1, bins], sin_ref[r : r + 1, bins]
                turned_re.append(re * cos - im * sin)
                turned_im.append(re * sin + im * cos)
            for k, turned in enumerate((turned_re, turned_im)):
                start = (2 * (g * PARTS + j) + k) * PIECE
                total += jnp.dot(
                    jnp.concatenate(turned).astype(jnp.bfloat16),
                    table_ref[start : start + PIECE],
                    preferred_element_type=jnp.float32,
                )
    total = total * (1.0 / math.sqrt(48 * F))
    for r in range(TURNS):
        width = min(SPAN, LAGS - r * SPAN)
        out_ref[:, r * SPAN : r * SPAN + width] = total[16 * r : 16 * (r + 1), :width]


def lag_sums(tables, got):
    return pl.pallas_call(
        lag_kernel,
        out_shape=jax.ShapeDtypeStruct((16, LAGS), jnp.float32),
        compiler_params=pltpu.CompilerParams(vmem_limit_bytes=32 * 1024 * 1024),
        name="lag_sums",
    )(*tables, *got)


def angles(freq, lag):
    turns = np.remainder((K0 + freq) * lag, SAMPLES)
    return turns * (2.0 * math.pi / SAMPLES)


def lag_tables():
    freq = np.arange(F, dtype=np.int64)
    turn = angles(freq, SPAN * np.arange(TURNS, dtype=np.int64)[:, None])
    near = angles(freq[:, None], np.arange(SPAN, dtype=np.int64) - HALF)
    near = near.reshape(CHUNKS * PARTS, PIECE, SPAN)
    table = np.stack([np.cos(near), -np.sin(near)], axis=1).reshape(2 * F, SPAN)
    return (
        np.cos(turn).astype(np.float32),
        np.sin(turn).astype(np.float32),
        table.astype(ml_dtypes.bfloat16),
    )


def on_device(tables, spectra, pair_list, pair_count):
    y, c = lax.axis_index("y"), lax.axis_index("c")
    me = (2 * y + c).reshape(1).astype(jnp.int32)
    z_count = lax.axis_size("z")
    z_up = [(n, (n + 1) % z_count) for n in range(z_count)]
    z_down = [((n + 1) % z_count, n) for n in range(z_count)]
    live = jnp.arange(128, dtype=jnp.int32)[None, None] < pair_count[:, None, None]
    first = 128 + pair_list[:, 0:1]
    second = pair_list[:, 1:2]
    second = jnp.where(second < 64, second + 128, jnp.where(second < 128, second, second - 128))
    rows = jnp.where(live, jnp.concatenate([first, second], axis=1), -1)
    yc_pairs = [[(n, n ^ m) for n in range(PARTS)] for m in range(PARTS)]
    rows = rows.reshape(1, 256)
    spectra, rows = lax.optimization_barrier((spectra, rows))
    near = [rows] + [lax.ppermute(rows, ("y", "c"), yc_pairs[m]) for m in (1, 2, 3)]
    near = jnp.concatenate(near)
    above = lax.ppermute(lax.dynamic_slice_in_dim(near, me[0], 1, 0), "z", z_down)
    is_first = (jnp.arange(256) < 128)[None]
    above = jnp.where(is_first | (above < 64), above, -1)
    column = jnp.arange(192, dtype=jnp.int32)
    picks = (jnp.concatenate([near, above])[:, :, None] == column).astype(jnp.bfloat16)

    arrived = []
    for chunk in range(CHUNKS):
        pieces = whiten(me, spectra, chunk)
        if chunk == 0:
            pieces, near = lax.optimization_barrier((pieces, near))
        arrived.append(
            [pieces[0]] + [lax.ppermute(pieces[m], ("y", "c"), yc_pairs[m]) for m in (2, 3, 1)]
        )
    crossed, moved = [], []
    for own, far, cross, side in arrived:
        blocks = [own, side, far, cross]
        top = jnp.where(y == 1, jnp.where(c == 1, own, side), jnp.where(c == 1, far, cross))
        low = jnp.where(y == 0, jnp.where(c == 0, own, side), jnp.where(c == 0, far, cross))
        moved.append(top)
        crossed.append(blocks + [lax.ppermute(top, "z", z_up), lax.ppermute(low, "z", z_down)])
    got = []
    for chunk in range(CHUNKS):
        other = pair_products((PARTS,), me, picks, crossed[chunk])
        below = lax.ppermute(other, "z", z_up)
        picks, other = lax.optimization_barrier((picks, other))
        product = pair_products(tuple(range(PARTS)), me, picks, crossed[chunk])
        product = product + jnp.pad(below, ((0, PARTS - 1), (0, 0), (0, 0)))
        product = product.reshape(PARTS * 128, 2 * PIECE)
        if chunk == 0:
            product, _ = lax.optimization_barrier((product, moved[1]))
        got.append(lax.all_to_all(product, ("y", "c", "h"), 0, 0, tiled=True).reshape(32, 16, 2 * PIECE))
    return lag_sums(tables, got)


def solution(mesh):
    inner = Mesh(mesh.devices.reshape(-1, 2, 2, 8), ("z", "y", "c", "h"))
    sta = ("z", "y", "c")
    tables = lag_tables()

    def run(spectra, pair_list, pair_count):
        return jax.shard_map(
            on_device,
            mesh=inner,
            in_specs=((P(),) * 3, P(sta, "h", None, None), P(sta, None, None), P(sta)),
            out_specs=P(sta + ("h",), None),
            check_vma=False,
        )(tuple(jnp.asarray(table) for table in tables), spectra, pair_list, pair_count)

    return run
```

```python
import functools
import math

import jax
import jax.numpy as jnp
import numpy as np
from jax import lax
from jax.experimental import pallas as pl
from jax.experimental.pallas import tpu as pltpu
from jax.sharding import Mesh
from jax.sharding import PartitionSpec as P
import ml_dtypes

F = 2048
BAND = 128
HALF = 1216
SAMPLES = 36000
K0 = 90
LAGS = 2432
SEGS = 6
CHUNKS = 2
PARTS = 4
WIDE = F // CHUNKS
PIECE = WIDE // PARTS
BANDS = PIECE // BAND
ROWS = 16
SPAN = 128
TURNS = -(-LAGS // SPAN)


def whiten_kernel(me_ref, x_ref, *out_refs):
    for m in range(PARTS):
        start = pl.multiple_of((me_ref[0] ^ m) * PIECE, PIECE)
        for s in range(SEGS):
            x = x_ref[:, s, :, pl.ds(start, PIECE)].astype(jnp.float32)
            re = x[:, 0, :]
            im = x[:, 1, :]
            for b in range(BANDS):
                a = re[:, b * BAND : (b + 1) * BAND]
                c = im[:, b * BAND : (b + 1) * BAND]
                power = jnp.sum(a * a + c * c, axis=-1, keepdims=True) / BAND
                gain = lax.rsqrt(power + 1e-06)
                lane = 2 * s * PIECE + b * BAND
                out_refs[m][:, lane : lane + BAND] = (a * gain).astype(jnp.bfloat16)
                lane += PIECE
                out_refs[m][:, lane : lane + BAND] = (c * gain).astype(jnp.bfloat16)


def whiten(me, spectra, chunk):
    stations = spectra.shape[0]
    width = 2 * SEGS * PIECE
    return pl.pallas_call(
        whiten_kernel,
        grid_spec=pltpu.PrefetchScalarGridSpec(
            num_scalar_prefetch=1,
            grid=(stations // ROWS,),
            in_specs=[pl.BlockSpec((ROWS, SEGS, 2, WIDE), lambda i, me: (i, 0, 0, chunk))],
            out_specs=[pl.BlockSpec((ROWS, width), lambda i, me: (i, 0))] * PARTS,
        ),
        out_shape=[jax.ShapeDtypeStruct((stations, width), jnp.bfloat16)] * PARTS,
        name="whiten",
    )(me, spectra)


def pair_kernel(numbers, me_ref, pick_ref, *refs):
    *sources, out_ref, held, sems = refs
    me = me_ref[0]
    places = [1 + (me ^ m) for m in range(PARTS)] + [5 - 5 * (me & 1), 5 * (me & 1)]
    needed = {place for j in numbers for place in range(max(j - 1, 0), j + 2)}
    if numbers == (PARTS,):
        needed.remove(PARTS)
    copies = []
    for n, (source, place) in enumerate(zip(sources, places)):
        wanted = functools.reduce(lambda a, b: a | b, [jnp.equal(place, p) for p in sorted(needed)])
        start = pl.multiple_of(place * 64, 64)
        copies.append((wanted, pltpu.make_async_copy(source, held.at[pl.ds(start, 64)], sems.at[n])))
    for wanted, copy in copies:
        pl.when(wanted)(copy.start)
    for wanted, copy in copies:
        pl.when(wanted)(copy.wait)
    for n, j in enumerate(numbers):
        if j == 0:
            pick, rows = pick_ref[me, :, 64:], slice(0, 128)
        else:
            pick = pick_ref[j ^ me if j < PARTS else PARTS]
            rows = slice((j - 1) * 64, (j + 2) * 64)
        cross_re = jnp.zeros((128, PIECE), jnp.float32)
        cross_im = jnp.zeros((128, PIECE), jnp.float32)
        for s in range(SEGS):
            lanes = slice(2 * s * PIECE, 2 * (s + 1) * PIECE)
            if j < PARTS:
                taken = jnp.dot(pick, held[rows, lanes], preferred_element_type=jnp.float32)
            else:
                taken = jnp.concatenate(
                    [
                        jnp.dot(pick[:128, 128:], held[320:384, lanes], preferred_element_type=jnp.float32),
                        jnp.dot(pick[128:, :64], held[192:256, lanes], preferred_element_type=jnp.float32),
                    ]
                )
            a_re, a_im = taken[:128, :PIECE], taken[:128, PIECE:]
            b_re, b_im = taken[128:, :PIECE], taken[128:, PIECE:]
            cross_re += a_re * b_re + a_im * b_im
            cross_im += a_im * b_re - a_re * b_im
        out_ref[n, :, :PIECE] = cross_re.astype(out_ref.dtype)
        out_ref[n, :, PIECE:] = cross_im.astype(out_ref.dtype)


def pair_products(numbers, me, picks, sources):
    width = 2 * SEGS * PIECE
    return pl.pallas_call(
        functools.partial(pair_kernel, numbers),
        in_specs=[
            pl.BlockSpec(memory_space=pltpu.SMEM),
            pl.BlockSpec(memory_space=pltpu.VMEM),
        ]
        + [pl.BlockSpec(memory_space=pltpu.HBM)] * 6,
        out_specs=pl.BlockSpec(memory_space=pltpu.VMEM),
        out_shape=jax.ShapeDtypeStruct((len(numbers), 128, 2 * PIECE), jnp.bfloat16),
        scratch_shapes=[
            pltpu.VMEM((6 * 64, width), jnp.bfloat16),
            pltpu.SemaphoreType.DMA((6,)),
        ],
        compiler_params=pltpu.CompilerParams(vmem_limit_bytes=32 * 1024 * 1024),
        name="pair_products",
    )(me, picks, *sources)


def lag_kernel(cos_ref, sin_ref, table_ref, *refs):
    got_refs, out_ref = refs[:-1], refs[-1]
    total = jnp.zeros((16 * TURNS, SPAN), jnp.float32)
    for g, got_ref in enumerate(got_refs):
        for j in range(PARTS):
            cross = got_ref[8 * j].astype(jnp.float32)
            for h in range(1, 8):
                cross += got_ref[8 * j + h].astype(jnp.float32)
            re, im = cross[:, :PIECE], cross[:, PIECE:]
            bins = slice((g * PARTS + j) * PIECE, (g * PARTS + j + 1) * PIECE)
            turned_re, turned_im = [], []
            for r in range(TURNS):
                cos, sin = cos_ref[r : r + 1, bins], sin_ref[r : r + 1, bins]
                turned_re.append(re * cos - im * sin)
                turned_im.append(re * sin + im * cos)
            for k, turned in enumerate((turned_re, turned_im)):
                start = (2 * (g * PARTS + j) + k) * PIECE
                total += jnp.dot(
                    jnp.concatenate(turned).astype(jnp.bfloat16),
                    table_ref[start : start + PIECE],
                    preferred_element_type=jnp.float32,
                )
    total = total * (1.0 / math.sqrt(48 * F))
    for r in range(TURNS):
        width = min(SPAN, LAGS - r * SPAN)
        out_ref[:, r * SPAN : r * SPAN + width] = total[16 * r : 16 * (r + 1), :width]


def lag_sums(tables, got):
    return pl.pallas_call(
        lag_kernel,
        out_shape=jax.ShapeDtypeStruct((16, LAGS), jnp.float32),
        compiler_params=pltpu.CompilerParams(vmem_limit_bytes=32 * 1024 * 1024),
        name="lag_sums",
    )(*tables, *got)


def angles(freq, lag):
    turns = np.remainder((K0 + freq) * lag, SAMPLES)
    return turns * (2.0 * math.pi / SAMPLES)


def lag_tables():
    freq = np.arange(F, dtype=np.int64)
    turn = angles(freq, SPAN * np.arange(TURNS, dtype=np.int64)[:, None])
    near = angles(freq[:, None], np.arange(SPAN, dtype=np.int64) - HALF)
    near = near.reshape(CHUNKS * PARTS, PIECE, SPAN)
    table = np.stack([np.cos(near), -np.sin(near)], axis=1).reshape(2 * F, SPAN)
    return (
        np.cos(turn).astype(np.float32),
        np.sin(turn).astype(np.float32),
        table.astype(ml_dtypes.bfloat16),
    )


def on_device(tables, spectra, pair_list, pair_count):
    y, c = lax.axis_index("y"), lax.axis_index("c")
    me = (2 * y + c).reshape(1).astype(jnp.int32)
    z_count = lax.axis_size("z")
    z_up = [(n, (n + 1) % z_count) for n in range(z_count)]
    z_down = [((n + 1) % z_count, n) for n in range(z_count)]
    zc = [(n, k) for n in range(z_count) for k in (0, 1)]
    one_way = [(2 * n + k, 2 * ((n + 2 * k - 1) % z_count) + k) for n, k in zc]
    other_way = [(2 * n + k, 2 * ((n + 1 - 2 * k) % z_count) + k) for n, k in zc]
    live = jnp.arange(128, dtype=jnp.int32)[None, None] < pair_count[:, None, None]
    first = 128 + pair_list[:, 0:1]
    second = pair_list[:, 1:2]
    second = jnp.where(second < 64, second + 128, jnp.where(second < 128, second, second - 128))
    rows = jnp.where(live, jnp.concatenate([first, second], axis=1), -1)
    yc_pairs = [[(n, n ^ m) for n in range(PARTS)] for m in range(PARTS)]
    rows = rows.reshape(1, 256)
    spectra, rows = lax.optimization_barrier((spectra, rows))
    near = [rows] + [lax.ppermute(rows, ("y", "c"), yc_pairs[m]) for m in (1, 2, 3)]
    near = jnp.concatenate(near)
    above = lax.ppermute(lax.dynamic_slice_in_dim(near, me[0], 1, 0), "z", z_down)
    is_first = (jnp.arange(256) < 128)[None]
    above = jnp.where(is_first | (above < 64), above, -1)
    column = jnp.arange(192, dtype=jnp.int32)
    picks = (jnp.concatenate([near, above])[:, :, None] == column).astype(jnp.bfloat16)

    arrived = []
    for chunk in range(CHUNKS):
        pieces = whiten(me, spectra, chunk)
        if chunk == 0:
            pieces, near, spectra = lax.optimization_barrier((pieces, near, spectra))
        arrived.append(
            [pieces[0]] + [lax.ppermute(pieces[m], ("y", "c"), yc_pairs[m]) for m in (2, 3, 1)]
        )
    products, moved = [], []
    for chunk in range(CHUNKS):
        own, far, cross, side = arrived[chunk]
        if chunk:
            product = products[-1][0]
            far, cross, side = [
                lax.optimization_barrier((block, product))[0] for block in (far, cross, side)
            ]
        moved.append(jnp.where(y == c, own, far))
        sources = [own, side, far, cross] + [
            lax.ppermute(moved[-1], ("z", "c"), one_way),
            lax.ppermute(jnp.where(y == c, cross, side), ("z", "c"), other_way),
        ]
        other = pair_products((PARTS,), me, picks, sources)
        below = lax.ppermute(other, "z", z_up)
        picks, other = lax.optimization_barrier((picks, other))
        products.append((pair_products(tuple(range(PARTS)), me, picks, sources), below))
    got = []
    for chunk, (product, below) in enumerate(products):
        product = product + jnp.pad(below, ((0, PARTS - 1), (0, 0), (0, 0)))
        product = product.reshape(PARTS * 128, 2 * PIECE)
        if chunk == 0:
            product, _ = lax.optimization_barrier((product, moved[1]))
        got.append(lax.all_to_all(product, ("y", "c", "h"), 0, 0, tiled=True).reshape(32, 16, 2 * PIECE))
    return lag_sums(tables, got)


def solution(mesh):
    inner = Mesh(mesh.devices.reshape(-1, 2, 2, 8), ("z", "y", "c", "h"))
    sta = ("z", "y", "c")
    tables = lag_tables()

    def run(spectra, pair_list, pair_count):
        return jax.shard_map(
            on_device,
            mesh=inner,
            in_specs=((P(),) * 3, P(sta, "h", None, None), P(sta, None, None), P(sta)),
            out_specs=P(sta + ("h",), None),
            check_vma=False,
        )(tuple(jnp.asarray(table) for table in tables), spectra, pair_list, pair_count)

    return run
```

```python
import functools
import math

import jax
import jax.numpy as jnp
import numpy as np
from jax import lax
from jax.experimental import pallas as pl
from jax.experimental.pallas import tpu as pltpu
from jax.sharding import Mesh
from jax.sharding import PartitionSpec as P
import ml_dtypes

F = 2048
BAND = 128
HALF = 1216
SAMPLES = 36000
K0 = 90
LAGS = 2432
SEGS = 6
CHUNKS = 2
PARTS = 4
WIDE = F // CHUNKS
PIECE = WIDE // PARTS
BANDS = PIECE // BAND
ROWS = 16
SPAN = 128
TURNS = -(-LAGS // SPAN)


def whiten_kernel(me_ref, x_ref, *out_refs):
    for m in range(PARTS):
        start = pl.multiple_of((me_ref[0] ^ m) * PIECE, PIECE)
        for s in range(SEGS):
            x = x_ref[:, s, :, pl.ds(start, PIECE)].astype(jnp.float32)
            re = x[:, 0, :]
            im = x[:, 1, :]
            for b in range(BANDS):
                a = re[:, b * BAND : (b + 1) * BAND]
                c = im[:, b * BAND : (b + 1) * BAND]
                power = jnp.sum(a * a + c * c, axis=-1, keepdims=True) / BAND
                gain = lax.rsqrt(power + 1e-06)
                lane = 2 * s * PIECE + b * BAND
                out_refs[m][:, lane : lane + BAND] = (a * gain).astype(jnp.bfloat16)
                lane += PIECE
                out_refs[m][:, lane : lane + BAND] = (c * gain).astype(jnp.bfloat16)


def whiten(me, spectra, chunk):
    stations = spectra.shape[0]
    width = 2 * SEGS * PIECE
    return pl.pallas_call(
        whiten_kernel,
        grid_spec=pltpu.PrefetchScalarGridSpec(
            num_scalar_prefetch=1,
            grid=(stations // ROWS,),
            in_specs=[pl.BlockSpec((ROWS, SEGS, 2, WIDE), lambda i, me: (i, 0, 0, chunk))],
            out_specs=[pl.BlockSpec((ROWS, width), lambda i, me: (i, 0))] * PARTS,
        ),
        out_shape=[jax.ShapeDtypeStruct((stations, width), jnp.bfloat16)] * PARTS,
        name="whiten",
    )(me, spectra)


def pair_kernel(numbers, me_ref, pick_ref, *refs):
    *sources, out_ref, held, sems = refs
    me = me_ref[0]
    places = [1 + (me ^ m) for m in range(PARTS)] + [5 - 5 * (me & 1), 5 * (me & 1)]
    needed = {place for j in numbers for place in range(max(j - 1, 0), j + 2)}
    if numbers == (PARTS,):
        needed.remove(PARTS)
    copies = []
    for n, (source, place) in enumerate(zip(sources, places)):
        wanted = functools.reduce(lambda a, b: a | b, [jnp.equal(place, p) for p in sorted(needed)])
        start = pl.multiple_of(place * 64, 64)
        copies.append((wanted, pltpu.make_async_copy(source, held.at[pl.ds(start, 64)], sems.at[n])))
    for wanted, copy in copies:
        pl.when(wanted)(copy.start)
    for wanted, copy in copies:
        pl.when(wanted)(copy.wait)
    for n, j in enumerate(numbers):
        if j == 0:
            pick, rows = pick_ref[me, :, 64:], slice(0, 128)
        else:
            pick = pick_ref[j ^ me if j < PARTS else PARTS]
            rows = slice((j - 1) * 64, (j + 2) * 64)
        cross_re = jnp.zeros((128, PIECE), jnp.float32)
        cross_im = jnp.zeros((128, PIECE), jnp.float32)
        for s in range(SEGS):
            lanes = slice(2 * s * PIECE, 2 * (s + 1) * PIECE)
            if j < PARTS:
                taken = jnp.dot(pick, held[rows, lanes], preferred_element_type=jnp.float32)
            else:
                taken = jnp.concatenate(
                    [
                        jnp.dot(pick[:128, 128:], held[320:384, lanes], preferred_element_type=jnp.float32),
                        jnp.dot(pick[128:, :64], held[192:256, lanes], preferred_element_type=jnp.float32),
                    ]
                )
            a_re, a_im = taken[:128, :PIECE], taken[:128, PIECE:]
            b_re, b_im = taken[128:, :PIECE], taken[128:, PIECE:]
            cross_re += a_re * b_re + a_im * b_im
            cross_im += a_im * b_re - a_re * b_im
        out_ref[n, :, :PIECE] = cross_re.astype(out_ref.dtype)
        out_ref[n, :, PIECE:] = cross_im.astype(out_ref.dtype)


def pair_products(numbers, me, picks, sources):
    width = 2 * SEGS * PIECE
    return pl.pallas_call(
        functools.partial(pair_kernel, numbers),
        in_specs=[
            pl.BlockSpec(memory_space=pltpu.SMEM),
            pl.BlockSpec(memory_space=pltpu.VMEM),
        ]
        + [pl.BlockSpec(memory_space=pltpu.HBM)] * 6,
        out_specs=pl.BlockSpec(memory_space=pltpu.VMEM),
        out_shape=jax.ShapeDtypeStruct((len(numbers), 128, 2 * PIECE), jnp.bfloat16),
        scratch_shapes=[
            pltpu.VMEM((6 * 64, width), jnp.bfloat16),
            pltpu.SemaphoreType.DMA((6,)),
        ],
        compiler_params=pltpu.CompilerParams(vmem_limit_bytes=32 * 1024 * 1024),
        name="pair_products",
    )(me, picks, *sources)


def lag_kernel(cos_ref, sin_ref, table_ref, *refs):
    got_refs, out_ref = refs[:-1], refs[-1]
    total = jnp.zeros((16 * TURNS, SPAN), jnp.float32)
    for g, got_ref in enumerate(got_refs):
        for j in range(PARTS):
            cross = got_ref[8 * j].astype(jnp.float32)
            for h in range(1, 8):
                cross += got_ref[8 * j + h].astype(jnp.float32)
            re, im = cross[:, :PIECE], cross[:, PIECE:]
            bins = slice((g * PARTS + j) * PIECE, (g * PARTS + j + 1) * PIECE)
            turned_re, turned_im = [], []
            for r in range(TURNS):
                cos, sin = cos_ref[r : r + 1, bins], sin_ref[r : r + 1, bins]
                turned_re.append(re * cos - im * sin)
                turned_im.append(re * sin + im * cos)
            for k, turned in enumerate((turned_re, turned_im)):
                start = (2 * (g * PARTS + j) + k) * PIECE
                total += jnp.dot(
                    jnp.concatenate(turned).astype(jnp.bfloat16),
                    table_ref[start : start + PIECE],
                    preferred_element_type=jnp.float32,
                )
    total = total * (1.0 / math.sqrt(48 * F))
    for r in range(TURNS):
        width = min(SPAN, LAGS - r * SPAN)
        out_ref[:, r * SPAN : r * SPAN + width] = total[16 * r : 16 * (r + 1), :width]


def lag_sums(tables, got):
    return pl.pallas_call(
        lag_kernel,
        out_shape=jax.ShapeDtypeStruct((16, LAGS), jnp.float32),
        compiler_params=pltpu.CompilerParams(vmem_limit_bytes=32 * 1024 * 1024),
        name="lag_sums",
    )(*tables, *got)


def angles(freq, lag):
    turns = np.remainder((K0 + freq) * lag, SAMPLES)
    return turns * (2.0 * math.pi / SAMPLES)


def lag_tables():
    freq = np.arange(F, dtype=np.int64)
    turn = angles(freq, SPAN * np.arange(TURNS, dtype=np.int64)[:, None])
    near = angles(freq[:, None], np.arange(SPAN, dtype=np.int64) - HALF)
    near = near.reshape(CHUNKS * PARTS, PIECE, SPAN)
    table = np.stack([np.cos(near), -np.sin(near)], axis=1).reshape(2 * F, SPAN)
    return (
        np.cos(turn).astype(np.float32),
        np.sin(turn).astype(np.float32),
        table.astype(ml_dtypes.bfloat16),
    )


def on_device(tables, spectra, pair_list, pair_count):
    y, c = lax.axis_index("y"), lax.axis_index("c")
    me = (2 * y + c).reshape(1).astype(jnp.int32)
    z_count = lax.axis_size("z")
    z_up = [(n, (n + 1) % z_count) for n in range(z_count)]
    z_down = [((n + 1) % z_count, n) for n in range(z_count)]
    zc = [(n, k) for n in range(z_count) for k in (0, 1)]
    one_way = [(2 * n + k, 2 * ((n + 2 * k - 1) % z_count) + k) for n, k in zc]
    other_way = [(2 * n + k, 2 * ((n + 1 - 2 * k) % z_count) + k) for n, k in zc]
    live = jnp.arange(128, dtype=jnp.int32)[None, None] < pair_count[:, None, None]
    first = 128 + pair_list[:, 0:1]
    second = pair_list[:, 1:2]
    second = jnp.where(second < 64, second + 128, jnp.where(second < 128, second, second - 128))
    rows = jnp.where(live, jnp.concatenate([first, second], axis=1), -1)
    yc_pairs = [[(n, n ^ m) for n in range(PARTS)] for m in range(PARTS)]
    rows = rows.reshape(1, 256)
    spectra, rows = lax.optimization_barrier((spectra, rows))
    near = [rows] + [lax.ppermute(rows, ("y", "c"), yc_pairs[m]) for m in (1, 2, 3)]
    near = jnp.concatenate(near)
    above = lax.ppermute(lax.dynamic_slice_in_dim(near, me[0], 1, 0), "z", z_down)
    is_first = (jnp.arange(256) < 128)[None]
    above = jnp.where(is_first | (above < 64), above, -1)
    column = jnp.arange(192, dtype=jnp.int32)
    picks = (jnp.concatenate([near, above])[:, :, None] == column).astype(jnp.bfloat16)

    arrived = []
    for chunk in range(CHUNKS):
        if chunk:
            spectra = lax.optimization_barrier((spectra, picks))[0]
        pieces = whiten(me, spectra, chunk)
        if chunk == 0:
            pieces, near, spectra = lax.optimization_barrier((pieces, near, spectra))
        arrived.append(
            [pieces[0]] + [lax.ppermute(pieces[m], ("y", "c"), yc_pairs[m]) for m in (2, 3, 1)]
        )
    products, moved = [], []
    for chunk in range(CHUNKS):
        own, far, cross, side = arrived[chunk]
        if chunk == 0:
            far = lax.optimization_barrier((far, arrived[1][0]))[0]
        else:
            product = products[-1][0]
            far, cross, side = [
                lax.optimization_barrier((block, product))[0] for block in (far, cross, side)
            ]
        moved.append(jnp.where(y == c, own, far))
        sources = [own, side, far, cross] + [
            lax.ppermute(moved[-1], ("z", "c"), one_way),
            lax.ppermute(jnp.where(y == c, cross, side), ("z", "c"), other_way),
        ]
        other = pair_products((PARTS,), me, picks, sources)
        below = lax.ppermute(other, "z", z_up)
        picks, other = lax.optimization_barrier((picks, other))
        products.append((pair_products(tuple(range(PARTS)), me, picks, sources), below))
    got = []
    for chunk, (product, below) in enumerate(products):
        product = product + jnp.pad(below, ((0, PARTS - 1), (0, 0), (0, 0)))
        product = product.reshape(PARTS * 128, 2 * PIECE)
        if chunk == 0:
            product, _ = lax.optimization_barrier((product, moved[1]))
        got.append(lax.all_to_all(product, ("y", "c", "h"), 0, 0, tiled=True).reshape(32, 16, 2 * PIECE))
    return lag_sums(tables, got)


def solution(mesh):
    inner = Mesh(mesh.devices.reshape(-1, 2, 2, 8), ("z", "y", "c", "h"))
    sta = ("z", "y", "c")
    tables = lag_tables()

    def run(spectra, pair_list, pair_count):
        return jax.shard_map(
            on_device,
            mesh=inner,
            in_specs=((P(),) * 3, P(sta, "h", None, None), P(sta, None, None), P(sta)),
            out_specs=P(sta + ("h",), None),
            check_vma=False,
        )(tuple(jnp.asarray(table) for table in tables), spectra, pair_list, pair_count)

    return run
```

```python
import functools
import math

import jax
import jax.numpy as jnp
import numpy as np
from jax import lax
from jax.experimental import pallas as pl
from jax.experimental.pallas import tpu as pltpu
from jax.sharding import Mesh
from jax.sharding import PartitionSpec as P
import ml_dtypes

F = 2048
BAND = 128
HALF = 1216
SAMPLES = 36000
K0 = 90
LAGS = 2432
SEGS = 6
CHUNKS = 2
PARTS = 4
WIDE = F // CHUNKS
PIECE = WIDE // PARTS
BANDS = PIECE // BAND
ROWS = 16
SPAN = 128
TURNS = -(-LAGS // SPAN)


def whiten_kernel(me_ref, x_ref, *out_refs):
    for m in range(PARTS):
        start = pl.multiple_of((me_ref[0] ^ m) * PIECE, PIECE)
        for s in range(SEGS):
            x = x_ref[:, s, :, pl.ds(start, PIECE)].astype(jnp.float32)
            re = x[:, 0, :]
            im = x[:, 1, :]
            for b in range(BANDS):
                a = re[:, b * BAND : (b + 1) * BAND]
                c = im[:, b * BAND : (b + 1) * BAND]
                power = jnp.sum(a * a + c * c, axis=-1, keepdims=True) / BAND
                gain = lax.rsqrt(power + 1e-06)
                lane = 2 * s * PIECE + b * BAND
                out_refs[m][:, lane : lane + BAND] = (a * gain).astype(jnp.bfloat16)
                lane += PIECE
                out_refs[m][:, lane : lane + BAND] = (c * gain).astype(jnp.bfloat16)


def whiten(me, spectra, chunk):
    stations = spectra.shape[0]
    width = 2 * SEGS * PIECE
    return pl.pallas_call(
        whiten_kernel,
        grid_spec=pltpu.PrefetchScalarGridSpec(
            num_scalar_prefetch=1,
            grid=(stations // ROWS,),
            in_specs=[pl.BlockSpec((ROWS, SEGS, 2, WIDE), lambda i, me: (i, 0, 0, chunk))],
            out_specs=[pl.BlockSpec((ROWS, width), lambda i, me: (i, 0))] * PARTS,
        ),
        out_shape=[jax.ShapeDtypeStruct((stations, width), jnp.bfloat16)] * PARTS,
        name="whiten",
    )(me, spectra)


def pair_kernel(numbers, me_ref, pick_ref, *refs):
    *sources, out_ref, held, sems = refs
    me = me_ref[0]
    places = [1 + (me ^ m) for m in range(PARTS)] + [5 - 5 * (me & 1), 5 * (me & 1)]
    needed = {place for j in numbers for place in range(max(j - 1, 0), j + 2)}
    if numbers == (PARTS,):
        needed.remove(PARTS)
    copies = []
    for n, (source, place) in enumerate(zip(sources, places)):
        wanted = functools.reduce(lambda a, b: a | b, [jnp.equal(place, p) for p in sorted(needed)])
        start = pl.multiple_of(place * 64, 64)
        copies.append((wanted, pltpu.make_async_copy(source, held.at[pl.ds(start, 64)], sems.at[n])))
    for wanted, copy in copies:
        pl.when(wanted)(copy.start)
    for wanted, copy in copies:
        pl.when(wanted)(copy.wait)
    for n, j in enumerate(numbers):
        if j == 0:
            pick, rows = pick_ref[me, :, 64:], slice(0, 128)
        else:
            pick = pick_ref[j ^ me if j < PARTS else PARTS]
            rows = slice((j - 1) * 64, (j + 2) * 64)
        cross_re = jnp.zeros((128, PIECE), jnp.float32)
        cross_im = jnp.zeros((128, PIECE), jnp.float32)
        for s in range(SEGS):
            lanes = slice(2 * s * PIECE, 2 * (s + 1) * PIECE)
            if j < PARTS:
                taken = jnp.dot(pick, held[rows, lanes], preferred_element_type=jnp.float32)
            else:
                taken = jnp.concatenate(
                    [
                        jnp.dot(pick[:128, 128:], held[320:384, lanes], preferred_element_type=jnp.float32),
                        jnp.dot(pick[128:, :64], held[192:256, lanes], preferred_element_type=jnp.float32),
                    ]
                )
            a_re, a_im = taken[:128, :PIECE], taken[:128, PIECE:]
            b_re, b_im = taken[128:, :PIECE], taken[128:, PIECE:]
            cross_re += a_re * b_re + a_im * b_im
            cross_im += a_im * b_re - a_re * b_im
        out_ref[n, :, :PIECE] = cross_re.astype(out_ref.dtype)
        out_ref[n, :, PIECE:] = cross_im.astype(out_ref.dtype)


def pair_products(numbers, me, picks, sources):
    width = 2 * SEGS * PIECE
    return pl.pallas_call(
        functools.partial(pair_kernel, numbers),
        in_specs=[
            pl.BlockSpec(memory_space=pltpu.SMEM),
            pl.BlockSpec(memory_space=pltpu.VMEM),
        ]
        + [pl.BlockSpec(memory_space=pltpu.HBM)] * 6,
        out_specs=pl.BlockSpec(memory_space=pltpu.VMEM),
        out_shape=jax.ShapeDtypeStruct((len(numbers), 128, 2 * PIECE), jnp.bfloat16),
        scratch_shapes=[
            pltpu.VMEM((6 * 64, width), jnp.bfloat16),
            pltpu.SemaphoreType.DMA((6,)),
        ],
        compiler_params=pltpu.CompilerParams(vmem_limit_bytes=32 * 1024 * 1024),
        name="pair_products",
    )(me, picks, *sources)


def lag_kernel(cos_ref, sin_ref, table_ref, *refs):
    got_refs, out_ref = refs[:-1], refs[-1]
    total = jnp.zeros((16 * TURNS, SPAN), jnp.float32)
    for g, got_ref in enumerate(got_refs):
        for j in range(PARTS):
            cross = got_ref[8 * j].astype(jnp.float32)
            for h in range(1, 8):
                cross += got_ref[8 * j + h].astype(jnp.float32)
            re, im = cross[:, :PIECE], cross[:, PIECE:]
            bins = slice((g * PARTS + j) * PIECE, (g * PARTS + j + 1) * PIECE)
            turned_re, turned_im = [], []
            for r in range(TURNS):
                cos, sin = cos_ref[r : r + 1, bins], sin_ref[r : r + 1, bins]
                turned_re.append(re * cos - im * sin)
                turned_im.append(re * sin + im * cos)
            for k, turned in enumerate((turned_re, turned_im)):
                start = (2 * (g * PARTS + j) + k) * PIECE
                total += jnp.dot(
                    jnp.concatenate(turned).astype(jnp.bfloat16),
                    table_ref[start : start + PIECE],
                    preferred_element_type=jnp.float32,
                )
    total = total * (1.0 / math.sqrt(48 * F))
    for r in range(TURNS):
        width = min(SPAN, LAGS - r * SPAN)
        out_ref[:, r * SPAN : r * SPAN + width] = total[16 * r : 16 * (r + 1), :width]


def lag_sums(tables, got):
    return pl.pallas_call(
        lag_kernel,
        out_shape=jax.ShapeDtypeStruct((16, LAGS), jnp.float32),
        compiler_params=pltpu.CompilerParams(vmem_limit_bytes=32 * 1024 * 1024),
        name="lag_sums",
    )(*tables, *got)


def angles(freq, lag):
    turns = np.remainder((K0 + freq) * lag, SAMPLES)
    return turns * (2.0 * math.pi / SAMPLES)


def lag_tables():
    freq = np.arange(F, dtype=np.int64)
    turn = angles(freq, SPAN * np.arange(TURNS, dtype=np.int64)[:, None])
    near = angles(freq[:, None], np.arange(SPAN, dtype=np.int64) - HALF)
    near = near.reshape(CHUNKS * PARTS, PIECE, SPAN)
    table = np.stack([np.cos(near), -np.sin(near)], axis=1).reshape(2 * F, SPAN)
    return (
        np.cos(turn).astype(np.float32),
        np.sin(turn).astype(np.float32),
        table.astype(ml_dtypes.bfloat16),
    )


def on_device(tables, spectra, pair_list, pair_count):
    y, c = lax.axis_index("y"), lax.axis_index("c")
    me = (2 * y + c).reshape(1).astype(jnp.int32)
    z_count = lax.axis_size("z")
    z_up = [(n, (n + 1) % z_count) for n in range(z_count)]
    z_down = [((n + 1) % z_count, n) for n in range(z_count)]
    zc = [(n, k) for n in range(z_count) for k in (0, 1)]
    one_way = [(2 * n + k, 2 * ((n + 2 * k - 1) % z_count) + k) for n, k in zc]
    other_way = [(2 * n + k, 2 * ((n + 1 - 2 * k) % z_count) + k) for n, k in zc]
    live = jnp.arange(128, dtype=jnp.int32)[None, None] < pair_count[:, None, None]
    first = 128 + pair_list[:, 0:1]
    second = pair_list[:, 1:2]
    second = jnp.where(second < 64, second + 128, jnp.where(second < 128, second, second - 128))
    rows = jnp.where(live, jnp.concatenate([first, second], axis=1), -1)
    yc_pairs = [[(n, n ^ m) for n in range(PARTS)] for m in range(PARTS)]
    rows = rows.reshape(1, 256)
    spectra, rows = lax.optimization_barrier((spectra, rows))
    near = [rows] + [lax.ppermute(rows, ("y", "c"), yc_pairs[m]) for m in (1, 2, 3)]
    near = jnp.concatenate(near)
    arrived = []
    for chunk in range(CHUNKS):
        pieces = whiten(me, spectra, chunk)
        if chunk == 0:
            pieces, near, spectra = lax.optimization_barrier((pieces, near, spectra))
        arrived.append(
            [pieces[0]] + [lax.ppermute(pieces[m], ("y", "c"), yc_pairs[m]) for m in (2, 3, 1)]
        )
    near = lax.optimization_barrier((near, arrived[1][0]))[0]
    above = lax.ppermute(lax.dynamic_slice_in_dim(near, me[0], 1, 0), "z", z_down)
    is_first = (jnp.arange(256) < 128)[None]
    above = jnp.where(is_first | (above < 64), above, -1)
    column = jnp.arange(192, dtype=jnp.int32)
    picks = (jnp.concatenate([near, above])[:, :, None] == column).astype(jnp.bfloat16)

    products, moved = [], []
    for chunk in range(CHUNKS):
        own, far, cross, side = arrived[chunk]
        if chunk:
            product = products[-1][0]
            far, cross, side = [
                lax.optimization_barrier((block, product))[0] for block in (far, cross, side)
            ]
        moved.append(jnp.where(y == c, own, far))
        sources = [own, side, far, cross] + [
            lax.ppermute(moved[-1], ("z", "c"), one_way),
            lax.ppermute(jnp.where(y == c, cross, side), ("z", "c"), other_way),
        ]
        other = pair_products((PARTS,), me, picks, sources)
        below = lax.ppermute(other, "z", z_up)
        picks, other = lax.optimization_barrier((picks, other))
        products.append((pair_products(tuple(range(PARTS)), me, picks, sources), below))
    got = []
    for chunk, (product, below) in enumerate(products):
        product = product + jnp.pad(below, ((0, PARTS - 1), (0, 0), (0, 0)))
        product = product.reshape(PARTS * 128, 2 * PIECE)
        if chunk == 0:
            product, _ = lax.optimization_barrier((product, moved[1]))
        got.append(lax.all_to_all(product, ("y", "c", "h"), 0, 0, tiled=True).reshape(32, 16, 2 * PIECE))
    return lag_sums(tables, got)


def solution(mesh):
    inner = Mesh(mesh.devices.reshape(-1, 2, 2, 8), ("z", "y", "c", "h"))
    sta = ("z", "y", "c")
    tables = lag_tables()

    def run(spectra, pair_list, pair_count):
        return jax.shard_map(
            on_device,
            mesh=inner,
            in_specs=((P(),) * 3, P(sta, "h", None, None), P(sta, None, None), P(sta)),
            out_specs=P(sta + ("h",), None),
            check_vma=False,
        )(tuple(jnp.asarray(table) for table in tables), spectra, pair_list, pair_count)

    return run
```
